128 devices in a mesh: dp: 16 (over x, z), ctx: 8 (over y, core).
Axes of the slice: x: 4, y: 4, z: 4, core: 2. Of those that a mesh axis runs over, the one named last changes fastest.
Arguments:
- tokens: bfloat16 [64, 5120, 1280], P('dp', 'ctx'), may hold values from -64 to 64
- router: bfloat16 [1280, 256], replicated, may hold values from -1 to 1
- expert_up: bfloat16 [128, 1280, 2560], P(('dp', 'ctx')), may hold values from -0.5 to 0.5
- expert_down: bfloat16 [128, 2560, 1280], P(('dp', 'ctx')), may hold values from -0.25 to 0.25
Outputs:
- mixed: bfloat16 [64, 5120, 1280], P('dp', 'ctx')
The draws below stay inside these ranges and needn't reach their ends.
All inputs are finite; a program needn't handle non-finite values.
Results may differ from the reference program's by a relative error of at most 0.015.
Values may be sent and summed in bfloat16 or wider, within the bound.
No kernel may reach another device: no remote copies, remote signals or barrier semaphores. Data moves between devices by JAX's collectives and lax.ppermute only.
A program may use at most 128 MiB of HBM per device.

```python
import math
import jax
import jax.numpy as jnp
from jax import lax

D = 1280
FF = 2560
PER_EXPERT = 2
TOK_DEV = 640
EXPERTS = 128
SLOTS = 256
CLIPS = 64
TOK = 5120
N_CTX = 8


def router_table(key):
    normal_draw = jax.random.normal(jax.random.fold_in(key, 7), (D, SLOTS), jnp.float32)
    lengths = jnp.sqrt(jnp.sum(normal_draw * normal_draw, axis=0))
    target = jnp.exp(jax.random.uniform(jax.random.fold_in(key, 8), (SLOTS,), jnp.float32, math.log(2.2), math.log(3.2)))
    return jnp.clip(normal_draw / lengths[None, :] * target[None, :], -1.0, 1.0)


def draw_router(key, part):
    return router_table(key).astype(jnp.bfloat16)


def draw_tokens(key, part):
    values = jnp.clip(jax.random.normal(jax.random.fold_in(key, 1), (CLIPS, TOK, D), jnp.float32), -6.0, 6.0)
    return values.astype(jnp.bfloat16)


def block_levels(key, dims, pieces, smallest, largest):
    def one(dim, blocks):
        steps = jax.random.uniform(jax.random.fold_in(jax.random.fold_in(key, 6), dim), (blocks,), jnp.float32, smallest / len(pieces), largest / len(pieces))
        return jnp.repeat(jnp.exp(steps), dims[dim] // blocks).reshape((-1,) + (1,) * (len(dims) - dim - 1))

    factor_of = one(*pieces[0])
    for cut in pieces[1:]:
        factor_of = factor_of * one(*cut)
    return factor_of


def noise(rng, shape, spread, bound, split=(), dtype=jnp.bfloat16):
    values = spread * jax.random.normal(rng, shape, jnp.float32)
    if split:
        values = values * block_levels(rng, shape, split, -0.22, 0.18)
    return jnp.clip(values, -bound, bound).astype(dtype)


def setup_inputs(seed: int = 0) -> dict:
    keys = jax.random.split(jax.random.key(seed), 5)
    tokens = draw_tokens(jax.random.fold_in(keys[4], 71), 0)
    router = draw_router(jax.random.fold_in(keys[4], 71), 0)
    expert_up = noise(keys[2], (EXPERTS, D, FF), (D // 9) ** -0.5, 0.5, ((0, 128),))
    expert_down = noise(keys[3], (EXPERTS, FF, D), (FF // 4) ** -0.5, 0.25, ((0, 128),))
    return {"tokens": tokens, "router": router, "expert_up": expert_up, "expert_down": expert_down}


def reference(tokens, router, expert_up, expert_down):
    def per_clip(clip_rows):
        logits = jnp.dot(clip_rows, router, preferred_element_type=jnp.float32)
        column_max = jnp.max(logits, axis=0)
        exponent = jnp.exp(logits - column_max[None, :])
        dispatch = (exponent / jnp.sum(exponent, axis=0)[None, :]).astype(jnp.bfloat16)
        blocks = jnp.einsum("btj,btd->bjd", dispatch.reshape(N_CTX, TOK_DEV, SLOTS).astype(jnp.float32), clip_rows.reshape(N_CTX, TOK_DEV, D).astype(jnp.float32))
        blocks = lax.optimization_barrier(blocks.astype(jnp.bfloat16)).astype(jnp.float32)
        slot_inputs = jnp.sum(blocks, axis=0).astype(jnp.bfloat16)
        row_max = jnp.max(logits, axis=1)
        row_exp = jnp.exp(logits - row_max[:, None])
        combine = (row_exp / jnp.sum(row_exp, axis=1)[:, None]).astype(jnp.bfloat16)
        return slot_inputs, combine

    slot_inputs, combine = lax.map(per_clip, tokens)
    grouped = jnp.moveaxis(slot_inputs.reshape(CLIPS, EXPERTS, PER_EXPERT, D), 1, 0)

    def per_expert(bundle):
        slot_rows, up_matrix, down_matrix = bundle
        flat = slot_rows.reshape(CLIPS * PER_EXPERT, D)
        hidden = jax.nn.gelu(jnp.dot(flat, up_matrix, preferred_element_type=jnp.float32), approximate=False).astype(jnp.bfloat16)
        produced = jnp.dot(hidden, down_matrix, preferred_element_type=jnp.float32).astype(jnp.bfloat16)
        return produced.reshape(CLIPS, PER_EXPERT, D)

    produced = lax.map(per_expert, (grouped, expert_up, expert_down))
    slot_outputs = jnp.moveaxis(produced, 0, 1).reshape(CLIPS, SLOTS, D)

    def per_mix(bundle):
        return jnp.dot(bundle[0], bundle[1], preferred_element_type=jnp.float32).astype(jnp.bfloat16)

    return lax.map(per_mix, (combine, slot_outputs))
```

```python
import functools

import jax
import jax.numpy as jnp
import numpy as np
from jax import lax
from jax.experimental import pallas as pl
from jax.experimental.pallas import tpu as pltpu
from jax.sharding import Mesh
from jax.sharding import PartitionSpec as P

F32, BF16 = jnp.float32, jnp.bfloat16
STAT = 128
CHIPS, PLACES, LINE, CORES = 64, 16, 4, 2
MIB = 1024 * 1024


def iota(shape, dim):
    return lax.broadcasted_iota(jnp.int32, shape, dim)


def pieces(value, count):
    out = []
    for _ in range(count):
        part = value.astype(BF16).astype(F32)
        out.append(part)
        value = value - part
    return out


def read_stats(stats):
    return stats[:, 0:1] + stats[:, 1:2] + stats[:, 2:3], stats[:, 3:4] + stats[:, 4:5]


def interleave(rows, back):
    new = iota((rows, rows), 1 if back else 0)
    old = iota((rows, rows), 0 if back else 1)
    place = (new // 2) % 4 * 32 + new // 8 * 2 + new % 2
    return jnp.where(old == place, 1.0, 0.0).astype(BF16)


def dispatch_kernel(core_ref, tokens_ref, router_ref, mine_ref, other_ref, logits_ref, ordered_ref):
    slots = router_ref.shape[1]
    half = slots // CORES

    @pl.when(pl.program_id(0) == 0)
    def _():
        row, column = iota((slots, slots), 0), iota((slots, slots), 1)
        core = core_ref[0]
        owner = jnp.where(column < half, core, 1 - core)
        within = column % half
        source = within // 2 * 4 + owner * 2 + within % 2
        chosen = jnp.where(row == source, 1.0, 0.0).astype(BF16)
        ordered_ref[...] = jnp.dot(router_ref[...], chosen, preferred_element_type=F32).astype(BF16)

    tokens = tokens_ref[0]
    logits = jnp.dot(tokens, ordered_ref[...], preferred_element_type=F32)
    logits_ref[0] = logits
    top = jnp.max(logits, axis=0, keepdims=True)
    exponent = jnp.exp(logits - top)
    total = jnp.sum(exponent, axis=0, keepdims=True)
    rows = pieces(top, 3) + pieces(total, 2) + [1.0 / total]
    rows.append(jnp.zeros((STAT - len(rows), slots), F32))
    stats = jnp.concatenate(rows, axis=0).T
    sums = lax.dot_general(exponent.astype(BF16), tokens, (((0,), (0,)), ((), ())), preferred_element_type=F32)
    sums = (sums * stats[:, 5:6]).astype(BF16)
    stats = stats.astype(BF16)
    depth = tokens.shape[1]
    mine_ref[0, :, :depth] = sums[:half]
    mine_ref[0, :, depth:] = stats[:half]
    other_ref[0, :, :depth] = sums[half:]
    other_ref[0, :, depth:] = stats[half:]


def combine_kernel(logits_ref, combine_ref):
    logits = logits_ref[0]
    exponent = jnp.exp(logits - jnp.max(logits, axis=1, keepdims=True))
    combine_ref[0] = (exponent / jnp.sum(exponent, axis=1, keepdims=True)).astype(BF16)


def merge_kernel(mine_ref, theirs_ref, out_ref):
    clips, part, width = mine_ref.shape
    depth = width - STAT
    rows = clips * part
    a = mine_ref[...].astype(F32).reshape(rows, width)
    b = theirs_ref[...].astype(F32).reshape(rows, width)
    top_a, total_a = read_stats(a[:, depth:])
    top_b, total_b = read_stats(b[:, depth:])
    top = jnp.maximum(top_a, top_b)
    weight_a = total_a * jnp.exp(top_a - top)
    weight_b = total_b * jnp.exp(top_b - top)
    total = weight_a + weight_b
    inverse = 1.0 / total
    sums = a[:, :depth] * (weight_a * inverse) + b[:, :depth] * (weight_b * inverse)
    lane = iota((rows, STAT), 1)
    stats = jnp.zeros((rows, STAT), F32)
    for k, value in enumerate(pieces(top, 3) + pieces(total, 2)):
        stats = jnp.where(lane == k, value, stats)
    order = interleave(rows, False)
    for lo, hi, value in ((0, depth, sums), (depth, width, stats)):
        moved = jnp.dot(order, value.astype(BF16), preferred_element_type=F32)
        out_ref[:, :, lo:hi] = moved.reshape(out_ref.shape[0], out_ref.shape[1], hi - lo).astype(BF16)


def expert_kernel(tile, received_ref, up_ref, down_ref, out_ref, rows_ref):
    depth = up_ref.shape[1]
    for place in range(PLACES):
        parts = [received_ref[place * LINE + y].astype(F32) for y in range(LINE)]
        stats = [read_stats(part[:, depth:]) for part in parts]
        top = functools.reduce(jnp.maximum, [s[0] for s in stats])
        weights = [s[1] * jnp.exp(s[0] - top) for s in stats]
        inverse = 1.0 / sum(weights)
        rows_ref[place * 8:place * 8 + 8, :] = sum(
            part[:, :depth] * (weight * inverse) for part, weight in zip(parts, weights)
        )
    rows = rows_ref[...].astype(BF16)
    result = jnp.zeros(rows.shape, F32)
    for start in range(0, up_ref.shape[2], tile):
        hidden = jnp.dot(rows, up_ref[0, :, start:start + tile], preferred_element_type=F32)
        hidden = (0.5 * hidden * (1.0 + lax.erf(hidden * np.float32(np.sqrt(0.5))))).astype(BF16)
        result = result + jnp.dot(hidden, down_ref[0, start:start + tile, :], preferred_element_type=F32)
    result = result.reshape(PLACES, 8, depth).astype(BF16)
    for place in range(PLACES):
        for y in range(LINE):
            out_ref[place * LINE + y] = result[place]


def mix_kernel(mine_ref, theirs_ref, combine_ref, out_ref, slots_ref):
    clips = slots_ref.shape[0]
    half = slots_ref.shape[1] // CORES
    depth = slots_ref.shape[2]

    @pl.when(pl.program_id(0) == 0)
    def _():
        order = interleave(128, True)
        for core, ref in enumerate((mine_ref, theirs_ref)):
            for group in range(CHIPS // 16):
                block = ref[group * 16:group * 16 + 16].astype(F32).reshape(128, depth).astype(BF16)
                moved = jnp.dot(order, block, preferred_element_type=F32).astype(BF16)
                for clip in range(clips):
                    at = core * half + group * 32
                    slots_ref[clip, at:at + 32, :] = moved[clip * 32:clip * 32 + 32]

    slots = slots_ref[pl.program_id(0)]
    out_ref[0] = jnp.dot(combine_ref[0], slots, preferred_element_type=F32).astype(BF16)


def params(mib):
    return pltpu.CompilerParams(vmem_limit_bytes=mib * MIB)


def shards(tokens, router, expert_up, expert_down):
    clips, count, depth = tokens.shape
    slots = router.shape[1]
    half = slots // CORES
    wide = depth + STAT
    hidden = expert_up.shape[2]
    core = lax.axis_index("core").astype(jnp.int32).reshape(1)
    swap = [(0, 1), (1, 0)]
    chips = ("x", "z", "y")

    mine, other, logits = pl.pallas_call(
        dispatch_kernel,
        grid=(clips,),
        in_specs=[
            pl.BlockSpec(memory_space=pltpu.SMEM),
            pl.BlockSpec((1, count, depth), lambda c: (c, 0, 0)),
            pl.BlockSpec((depth, slots), lambda c: (0, 0)),
        ],
        out_specs=[
            pl.BlockSpec((1, half, wide), lambda c: (c, 0, 0)),
            pl.BlockSpec((1, half, wide), lambda c: (c, 0, 0)),
            pl.BlockSpec((1, count, slots), lambda c: (c, 0, 0)),
        ],
        out_shape=[
            jax.ShapeDtypeStruct((clips, half, wide), BF16),
            jax.ShapeDtypeStruct((clips, half, wide), BF16),
            jax.ShapeDtypeStruct((clips, count, slots), F32),
        ],
        scratch_shapes=[pltpu.VMEM((depth, slots), BF16)],
        compiler_params=params(24),
    )(core, tokens, router)

    theirs = lax.ppermute(other, "core", swap)

    merged = pl.pallas_call(
        merge_kernel,
        grid=(CHIPS // 16,),
        in_specs=[pl.BlockSpec((clips, 32, wide), lambda g: (0, g, 0))] * 2,
        out_specs=pl.BlockSpec((16, 8, wide), lambda g: (g, 0, 0)),
        out_shape=jax.ShapeDtypeStruct((CHIPS, 8, wide), BF16),
        compiler_params=params(16),
    )(mine, theirs)

    received = lax.all_to_all(merged, chips, 0, 0, tiled=False)

    combine = pl.pallas_call(
        combine_kernel,
        grid=(clips,),
        in_specs=[pl.BlockSpec((1, count, slots), lambda c: (c, 0, 0))],
        out_specs=pl.BlockSpec((1, count, slots), lambda c: (c, 0, 0)),
        out_shape=jax.ShapeDtypeStruct((clips, count, slots), BF16),
        compiler_params=params(12),
    )(logits)

    whole = pl.BlockSpec(memory_space=pltpu.VMEM)
    results = pl.pallas_call(
        functools.partial(expert_kernel, 512),
        in_specs=[whole] * 3,
        out_specs=whole,
        out_shape=jax.ShapeDtypeStruct((CHIPS, 8, depth), BF16),
        scratch_shapes=[pltpu.VMEM((PLACES * 8, depth), F32)],
        compiler_params=params(32),
    )(received, expert_up, expert_down)

    returned = lax.all_to_all(results, chips, 0, 0, tiled=False)
    partner = lax.ppermute(returned, "core", swap)

    full = pl.BlockSpec((CHIPS, 8, depth), lambda c: (0, 0, 0))
    return pl.pallas_call(
        mix_kernel,
        grid=(clips,),
        in_specs=[full, full, pl.BlockSpec((1, count, slots), lambda c: (c, 0, 0))],
        out_specs=pl.BlockSpec((1, count, depth), lambda c: (c, 0, 0)),
        out_shape=jax.ShapeDtypeStruct((clips, count, depth), BF16),
        scratch_shapes=[pltpu.VMEM((clips, slots, depth), BF16)],
        compiler_params=params(32),
    )(returned, partner, combine)


def solution(mesh):
    fine = Mesh(np.asarray(mesh.devices).reshape(4, 4, LINE, CORES), ("x", "z", "y", "core"))
    in_specs = (
        P(("x", "z"), ("y", "core"), None),
        P(),
        P(("x", "z", "y", "core"), None, None),
        P(("x", "z", "y", "core"), None, None),
    )
    out_specs = P(("x", "z"), ("y", "core"), None)
    return jax.shard_map(shards, mesh=fine, in_specs=in_specs, out_specs=out_specs, check_vma=False)
```

```python
import functools

import jax
import jax.numpy as jnp
import numpy as np
from jax import lax
from jax.experimental import pallas as pl
from jax.experimental.pallas import tpu as pltpu
from jax.sharding import Mesh
from jax.sharding import PartitionSpec as P

F32, BF16 = jnp.float32, jnp.bfloat16
STAT = 128
CHIPS, PLACES, LINE, CORES = 64, 16, 4, 2
MIB = 1024 * 1024


def iota(shape, dim):
    return lax.broadcasted_iota(jnp.int32, shape, dim)


def pieces(value, count):
    out = []
    for _ in range(count):
        part = value.astype(BF16).astype(F32)
        out.append(part)
        value = value - part
    return out


def read_stats(stats):
    return stats[:, 0:1] + stats[:, 1:2] + stats[:, 2:3], stats[:, 3:4] + stats[:, 4:5]


def interleave(rows, back):
    new = iota((rows, rows), 1 if back else 0)
    old = iota((rows, rows), 0 if back else 1)
    place = (new // 2) % 4 * (rows // 4) + new // 8 * 2 + new % 2
    return jnp.where(old == place, 1.0, 0.0).astype(BF16)


def dispatch_kernel(
    core_ref, tokens_hbm, router_ref, mine_ref, other_ref, combine_ref, tokens_ref, ordered_ref, sems
):
    clips, _, depth = tokens_ref.shape
    slots = router_ref.shape[1]
    half = slots // CORES
    fetches = [pltpu.make_async_copy(tokens_hbm.at[c], tokens_ref.at[c], sems.at[c]) for c in range(clips)]
    for copy in fetches:
        copy.start()
    row, column = iota((slots, slots), 0), iota((slots, slots), 1)
    core = core_ref[0]
    owner = jnp.where(column < half, core, 1 - core)
    within = column % half
    source = within // 2 * 4 + owner * 2 + within % 2
    chosen = jnp.where(row == source, 1.0, 0.0).astype(BF16)
    ordered_ref[...] = jnp.dot(router_ref[...], chosen, preferred_element_type=F32).astype(BF16)

    def scores(c):
        fetches[c].wait()
        return jnp.dot(tokens_ref[c], ordered_ref[...], preferred_element_type=F32)

    def over_tokens(logits):
        top = jnp.max(logits, axis=0, keepdims=True)
        exponent = jnp.exp(logits - top)
        total = jnp.sum(exponent, axis=0, keepdims=True)
        rows = pieces(top, 3) + pieces(total, 2) + [1.0 / total]
        rows.append(jnp.zeros((STAT - len(rows), slots), F32))
        return exponent.astype(BF16), jnp.concatenate(rows, axis=0).T

    def over_slots(c, logits):
        exponent = jnp.exp(logits - jnp.max(logits, axis=1, keepdims=True))
        combine_ref[c] = (exponent * (1.0 / jnp.sum(exponent, axis=1, keepdims=True))).astype(BF16)

    def sums(c, exponent, stats):
        value = lax.dot_general(exponent, tokens_ref[c], (((0,), (0,)), ((), ())), preferred_element_type=F32)
        value = (value * stats[:, 5:6]).astype(BF16)
        stats = stats.astype(BF16)
        mine_ref[c, :, :depth] = value[:half]
        mine_ref[c, :, depth:] = stats[:half]
        other_ref[c, :, :depth] = value[half:]
        other_ref[c, :, depth:] = stats[half:]

    ahead, ready = scores(0), None
    for c in range(clips):
        logits = ahead
        if c + 1 < clips:
            ahead = scores(c + 1)
        fresh = over_tokens(logits)
        over_slots(c, logits)
        if ready is not None:
            sums(c - 1, *ready)
        ready = fresh
    sums(clips - 1, *ready)


def merge_kernel(mine_ref, theirs_ref, out_ref):
    clips, half, width = mine_ref.shape
    depth = width - STAT
    rows, part = 256, 256 // clips
    order = interleave(rows, False)
    for group in range(half // part):
        at = slice(group * part, group * part + part)
        to = slice(group * rows // 8, (group + 1) * rows // 8)

        def load(ref, lo, hi):
            return ref[:, at, lo:hi].astype(F32).reshape(rows, hi - lo)

        def store(lo, hi, value):
            moved = jnp.dot(order, value.astype(BF16), preferred_element_type=F32)
            out_ref[to, :, lo:hi] = moved.reshape(rows // 8, 8, hi - lo).astype(BF16)

        top_a, total_a = read_stats(load(mine_ref, depth, width))
        top_b, total_b = read_stats(load(theirs_ref, depth, width))
        top = jnp.maximum(top_a, top_b)
        weight_a = total_a * jnp.exp(top_a - top)
        weight_b = total_b * jnp.exp(top_b - top)
        total = weight_a + weight_b
        inverse = 1.0 / total
        lane = iota((rows, STAT), 1)
        stats = jnp.zeros((rows, STAT), F32)
        for k, value in enumerate(pieces(top, 3) + pieces(total, 2)):
            stats = jnp.where(lane == k, value, stats)
        store(depth, width, stats)
        weight_a, weight_b = weight_a * inverse, weight_b * inverse
        for lo in range(0, depth, 256):
            hi = lo + 256
            store(lo, hi, load(mine_ref, lo, hi) * weight_a + load(theirs_ref, lo, hi) * weight_b)


def expert_kernel(tile, received_ref, up_ref, down_ref, out_ref, rows_ref):
    depth = up_ref.shape[1]
    for place in range(PLACES):
        parts = [received_ref[place * LINE + y].astype(F32) for y in range(LINE)]
        stats = [read_stats(part[:, depth:]) for part in parts]
        top = functools.reduce(jnp.maximum, [s[0] for s in stats])
        weights = [s[1] * jnp.exp(s[0] - top) for s in stats]
        inverse = 1.0 / sum(weights)
        rows_ref[place * 8:place * 8 + 8, :] = sum(
            part[:, :depth] * (weight * inverse) for part, weight in zip(parts, weights)
        )
    rows = rows_ref[...].astype(BF16)
    result = jnp.zeros(rows.shape, F32)
    for start in range(0, up_ref.shape[2], tile):
        hidden = jnp.dot(rows, up_ref[0, :, start:start + tile], preferred_element_type=F32)
        hidden = (0.5 * hidden * (1.0 + lax.erf(hidden * np.float32(np.sqrt(0.5))))).astype(BF16)
        result = result + jnp.dot(hidden, down_ref[0, start:start + tile, :], preferred_element_type=F32)
    result = result.reshape(PLACES, 8, depth).astype(BF16)
    for place in range(PLACES):
        for y in range(LINE):
            out_ref[place * LINE + y] = result[place]


def by_clip(ref, out_ref):
    chips, lines, depth = ref.shape
    rows = 256
    order = interleave(rows, True)
    clips, part = 4, rows // 4
    for group in range(chips * lines // rows):
        for lo in range(0, depth, 256):
            block = ref[group * rows // 8:(group + 1) * rows // 8, :, lo:lo + 256]
            block = block.astype(F32).reshape(rows, 256).astype(BF16)
            moved = jnp.dot(order, block, preferred_element_type=F32).astype(BF16)
            out_ref[:, group * part:group * part + part, lo:lo + 256] = moved.reshape(clips, part, 256)


def mix_kernel(tile, mine_ref, theirs_ref, combine_ref, out_hbm, slots_ref, out_ref, sems):
    by_clip(theirs_ref, slots_ref)
    copies = []
    for c in range(combine_ref.shape[0]):
        slots = jnp.concatenate([mine_ref[c], slots_ref[c]], axis=0)
        for lo in range(0, combine_ref.shape[1], tile):
            out_ref[c, lo:lo + tile] = jnp.dot(
                combine_ref[c, lo:lo + tile], slots, preferred_element_type=F32
            ).astype(BF16)
            at = pl.ds(lo, tile)
            copy = pltpu.make_async_copy(out_ref.at[c, at], out_hbm.at[c, at], sems.at[len(copies)])
            copy.start()
            copies.append(copy)
    for copy in copies:
        copy.wait()


def params(mib):
    return pltpu.CompilerParams(vmem_limit_bytes=mib * MIB)


def shards(tokens, router, expert_up, expert_down):
    clips, count, depth = tokens.shape
    slots = router.shape[1]
    half = slots // CORES
    wide = depth + STAT
    core = lax.axis_index("core").astype(jnp.int32).reshape(1)
    swap = [(0, 1), (1, 0)]
    chips = ("x", "z", "y")

    whole = pl.BlockSpec(memory_space=pltpu.VMEM)
    far = pl.BlockSpec(memory_space=pltpu.HBM)

    mine, other, combine = pl.pallas_call(
        dispatch_kernel,
        in_specs=[pl.BlockSpec(memory_space=pltpu.SMEM), far, whole],
        out_specs=[whole] * 3,
        out_shape=[
            jax.ShapeDtypeStruct((clips, half, wide), BF16),
            jax.ShapeDtypeStruct((clips, half, wide), BF16),
            jax.ShapeDtypeStruct((clips, count, slots), BF16),
        ],
        scratch_shapes=[
            pltpu.VMEM((clips, count, depth), BF16),
            pltpu.VMEM((depth, slots), BF16),
            pltpu.SemaphoreType.DMA((clips,)),
        ],
        compiler_params=params(48),
    )(core, tokens, router)

    theirs = lax.ppermute(other, "core", swap)

    merged = pl.pallas_call(
        merge_kernel,
        in_specs=[whole] * 2,
        out_specs=whole,
        out_shape=jax.ShapeDtypeStruct((CHIPS, 8, wide), BF16),
        compiler_params=params(16),
    )(mine, theirs)

    received = lax.all_to_all(merged, chips, 0, 0, tiled=False)

    results = pl.pallas_call(
        functools.partial(expert_kernel, 512),
        in_specs=[whole] * 3,
        out_specs=whole,
        out_shape=jax.ShapeDtypeStruct((CHIPS, 8, depth), BF16),
        scratch_shapes=[pltpu.VMEM((PLACES * 8, depth), F32)],
        compiler_params=params(32),
    )(received, expert_up, expert_down)

    returned = lax.all_to_all(results, chips, 0, 0, tiled=False)
    partner = lax.ppermute(returned, "core", swap)

    own = pl.pallas_call(
        by_clip,
        in_specs=[whole],
        out_specs=whole,
        out_shape=jax.ShapeDtypeStruct((clips, half, depth), BF16),
        compiler_params=params(16),
    )(returned)

    tile = count // 2
    return pl.pallas_call(
        functools.partial(mix_kernel, tile),
        in_specs=[whole] * 3,
        out_specs=far,
        out_shape=jax.ShapeDtypeStruct((clips, count, depth), BF16),
        scratch_shapes=[
            pltpu.VMEM((clips, half, depth), BF16),
            pltpu.VMEM((clips, count, depth), BF16),
            pltpu.SemaphoreType.DMA((clips * 2,)),
        ],
        compiler_params=params(24),
    )(own, partner, combine)


def solution(mesh):
    fine = Mesh(np.asarray(mesh.devices).reshape(4, 4, LINE, CORES), ("x", "z", "y", "core"))
    in_specs = (
        P(("x", "z"), ("y", "core"), None),
        P(),
        P(("x", "z", "y", "core"), None, None),
        P(("x", "z", "y", "core"), None, None),
    )
    out_specs = P(("x", "z"), ("y", "core"), None)
    return jax.shard_map(shards, mesh=fine, in_specs=in_specs, out_specs=out_specs, check_vma=False)
```

```python
import functools

import jax
import jax.numpy as jnp
import numpy as np
from jax import lax
from jax.experimental import pallas as pl
from jax.experimental.pallas import tpu as pltpu
from jax.sharding import Mesh
from jax.sharding import PartitionSpec as P

F32, BF16 = jnp.float32, jnp.bfloat16
STAT = 128
CHIPS, PLACES, LINE, CORES = 64, 16, 4, 2
MIB = 1024 * 1024


def iota(shape, dim):
    return lax.broadcasted_iota(jnp.int32, shape, dim)


def pieces(value, count):
    out = []
    for _ in range(count):
        part = value.astype(BF16).astype(F32)
        out.append(part)
        value = value - part
    return out


def read_stats(stats):
    return stats[:, 0:1] + stats[:, 1:2] + stats[:, 2:3], stats[:, 3:4] + stats[:, 4:5]


def interleave(rows, back):
    new = iota((rows, rows), 1 if back else 0)
    old = iota((rows, rows), 0 if back else 1)
    place = (new // 2) % 4 * (rows // 4) + new // 8 * 2 + new % 2
    return jnp.where(old == place, 1.0, 0.0).astype(BF16)


def stats_columns(logits):
    top = jnp.max(logits, axis=0, keepdims=True)
    exponent = jnp.exp(logits - top)
    total = jnp.sum(exponent, axis=0, keepdims=True)
    rows = pieces(top, 3) + pieces(total, 2) + [1.0 / total]
    rows.append(jnp.zeros((STAT - len(rows), logits.shape[1]), F32))
    return exponent.astype(BF16), jnp.concatenate(rows, axis=0).T


def store_sums(out_ref, c, exponent, stats, tokens):
    depth = tokens.shape[1]
    value = lax.dot_general(exponent, tokens, (((0,), (0,)), ((), ())), preferred_element_type=F32)
    out_ref[c, :, :depth] = (value * stats[:, 5:6]).astype(BF16)
    out_ref[c, :, depth:] = stats.astype(BF16)


def scores_kernel(
    core_ref, tokens_hbm, router_ref, other_ref, tokens_ref, logits_ref, ordered_ref, sems
):
    clips = tokens_ref.shape[0]
    slots = router_ref.shape[1]
    half = slots // CORES
    fetches = [pltpu.make_async_copy(tokens_hbm.at[c], tokens_ref.at[c], sems.at[c]) for c in range(clips)]
    for copy in fetches:
        copy.start()
    row, column = iota((slots, slots), 0), iota((slots, slots), 1)
    core = core_ref[0]
    owner = jnp.where(column < half, core, 1 - core)
    within = column % half
    source = within // 2 * 4 + owner * 2 + within % 2
    chosen = jnp.where(row == source, 1.0, 0.0).astype(BF16)
    ordered_ref[...] = jnp.dot(router_ref[...], chosen, preferred_element_type=F32).astype(BF16)

    def scores(c):
        logits_ref[c] = jnp.dot(tokens_ref[c], ordered_ref[...], preferred_element_type=F32)

    def rest(c):
        store_sums(other_ref, c, *stats_columns(logits_ref[c, :, half:]), tokens_ref[c])

    for copy in fetches[:2]:
        copy.wait()
    scores(0)
    scores(1)
    rest(0)
    for copy in fetches[2:]:
        copy.wait()
    scores(2)
    rest(1)
    scores(3)
    rest(2)
    rest(3)


def sums_kernel(tokens_ref, logits_ref, mine_ref, combine_ref):
    half = mine_ref.shape[1]
    for c in range(tokens_ref.shape[0]):
        logits = logits_ref[c]
        store_sums(mine_ref, c, *stats_columns(logits[:, :half]), tokens_ref[c])
        exponent = jnp.exp(logits - jnp.max(logits, axis=1, keepdims=True))
        combine_ref[c] = (exponent * (1.0 / jnp.sum(exponent, axis=1, keepdims=True))).astype(BF16)


def merge_kernel(mine_ref, theirs_ref, out_ref):
    clips, half, width = mine_ref.shape
    depth = width - STAT
    rows, part = 256, 256 // clips
    order = interleave(rows, False)
    for group in range(half // part):
        at = slice(group * part, group * part + part)
        to = slice(group * rows // 8, (group + 1) * rows // 8)

        def load(ref, lo, hi):
            return ref[:, at, lo:hi].astype(F32).reshape(rows, hi - lo)

        def store(lo, hi, value):
            moved = jnp.dot(order, value.astype(BF16), preferred_element_type=F32)
            out_ref[to, :, lo:hi] = moved.reshape(rows // 8, 8, hi - lo).astype(BF16)

        top_a, total_a = read_stats(load(mine_ref, depth, width))
        top_b, total_b = read_stats(load(theirs_ref, depth, width))
        top = jnp.maximum(top_a, top_b)
        weight_a = total_a * jnp.exp(top_a - top)
        weight_b = total_b * jnp.exp(top_b - top)
        total = weight_a + weight_b
        inverse = 1.0 / total
        lane = iota((rows, STAT), 1)
        stats = jnp.zeros((rows, STAT), F32)
        for k, value in enumerate(pieces(top, 3) + pieces(total, 2)):
            stats = jnp.where(lane == k, value, stats)
        store(depth, width, stats)
        weight_a, weight_b = weight_a * inverse, weight_b * inverse
        for lo in range(0, depth, 256):
            hi = lo + 256
            store(lo, hi, load(mine_ref, lo, hi) * weight_a + load(theirs_ref, lo, hi) * weight_b)


def expert_kernel(tile, received_ref, up_ref, down_ref, out_ref, rows_ref, hidden_ref):
    depth, hidden = up_ref.shape[1:]
    for place in range(PLACES):
        parts = [received_ref[place * LINE + y].astype(F32) for y in range(LINE)]
        stats = [read_stats(part[:, depth:]) for part in parts]
        top = functools.reduce(jnp.maximum, [s[0] for s in stats])
        weights = [s[1] * jnp.exp(s[0] - top) for s in stats]
        inverse = 1.0 / sum(weights)
        rows_ref[place * 8:place * 8 + 8, :] = sum(
            part[:, :depth] * (weight * inverse) for part, weight in zip(parts, weights)
        )
    rows = rows_ref[...].astype(BF16)
    for lo in range(0, hidden, 2 * tile):
        hi = lo + 2 * tile
        value = jnp.dot(rows, up_ref[0, :, lo:hi], preferred_element_type=F32)
        hidden_ref[:, lo:hi] = (0.5 * value * (1.0 + lax.erf(value * np.float32(np.sqrt(0.5))))).astype(BF16)
    for lo in range(0, depth, tile):
        hi = lo + tile
        result = jnp.dot(hidden_ref[...], down_ref[0, :, lo:hi], preferred_element_type=F32)
        result = result.reshape(PLACES, 8, tile).astype(BF16)
        for place in range(PLACES):
            for y in range(LINE):
                out_ref[place * LINE + y, :, lo:hi] = result[place]


def by_clip(ref, out_ref):
    chips, lines, depth = ref.shape
    rows = 256
    order = interleave(rows, True)
    clips, part = 4, rows // 4
    for group in range(chips * lines // rows):
        for lo in range(0, depth, 256):
            block = ref[group * rows // 8:(group + 1) * rows // 8, :, lo:lo + 256]
            block = block.astype(F32).reshape(rows, 256).astype(BF16)
            moved = jnp.dot(order, block, preferred_element_type=F32).astype(BF16)
            out_ref[:, group * part:group * part + part, lo:lo + 256] = moved.reshape(clips, part, 256)


def mix_kernel(tile, mine_ref, theirs_ref, combine_ref, out_hbm, slots_ref, out_ref, sems):
    by_clip(theirs_ref, slots_ref)
    copies = []
    for c in range(combine_ref.shape[0]):
        slots = jnp.concatenate([mine_ref[c], slots_ref[c]], axis=0)
        for lo in range(0, combine_ref.shape[1], tile):
            out_ref[c, lo:lo + tile] = jnp.dot(
                combine_ref[c, lo:lo + tile], slots, preferred_element_type=F32
            ).astype(BF16)
            at = pl.ds(lo, tile)
            copy = pltpu.make_async_copy(out_ref.at[c, at], out_hbm.at[c, at], sems.at[len(copies)])
            copy.start()
            copies.append(copy)
    for copy in copies:
        copy.wait()


def params(mib):
    return pltpu.CompilerParams(vmem_limit_bytes=mib * MIB)


def shards(tokens, router, expert_up, expert_down):
    clips, count, depth = tokens.shape
    slots = router.shape[1]
    half = slots // CORES
    wide = depth + STAT
    core = lax.axis_index("core").astype(jnp.int32).reshape(1)
    swap = [(0, 1), (1, 0)]
    chips = ("x", "z", "y")

    whole = pl.BlockSpec(memory_space=pltpu.VMEM)
    far = pl.BlockSpec(memory_space=pltpu.HBM)

    other, near, logits = pl.pallas_call(
        scores_kernel,
        in_specs=[pl.BlockSpec(memory_space=pltpu.SMEM), far, whole],
        out_specs=[whole] * 3,
        out_shape=[
            jax.ShapeDtypeStruct((clips, half, wide), BF16),
            jax.ShapeDtypeStruct((clips, count, depth), BF16),
            jax.ShapeDtypeStruct((clips, count, slots), F32),
        ],
        scratch_shapes=[pltpu.VMEM((depth, slots), BF16), pltpu.SemaphoreType.DMA((clips,))],
        compiler_params=params(39),
    )(core, tokens, router)

    theirs = lax.ppermute(other, "core", swap)

    mine, combine = pl.pallas_call(
        sums_kernel,
        in_specs=[whole] * 2,
        out_specs=[whole] * 2,
        out_shape=[
            jax.ShapeDtypeStruct((clips, half, wide), BF16),
            jax.ShapeDtypeStruct((clips, count, slots), BF16),
        ],
        compiler_params=params(16),
    )(near, logits)

    merged = pl.pallas_call(
        merge_kernel,
        in_specs=[whole] * 2,
        out_specs=whole,
        out_shape=jax.ShapeDtypeStruct((CHIPS, 8, wide), BF16),
        compiler_params=params(16),
    )(mine, theirs)

    received = lax.all_to_all(merged, chips, 0, 0, tiled=False)

    results = pl.pallas_call(
        functools.partial(expert_kernel, 256),
        in_specs=[whole] * 3,
        out_specs=whole,
        out_shape=jax.ShapeDtypeStruct((CHIPS, 8, depth), BF16),
        scratch_shapes=[pltpu.VMEM((PLACES * 8, depth), F32), pltpu.VMEM((PLACES * 8, expert_up.shape[2]), BF16)],
        compiler_params=params(32),
    )(received, expert_up, expert_down)

    returned = lax.all_to_all(results, chips, 0, 0, tiled=False)
    partner = lax.ppermute(returned, "core", swap)

    own = pl.pallas_call(
        by_clip,
        in_specs=[whole],
        out_specs=whole,
        out_shape=jax.ShapeDtypeStruct((clips, half, depth), BF16),
        compiler_params=params(16),
    )(returned)

    tile = count // 2
    return pl.pallas_call(
        functools.partial(mix_kernel, tile),
        in_specs=[whole] * 3,
        out_specs=far,
        out_shape=jax.ShapeDtypeStruct((clips, count, depth), BF16),
        scratch_shapes=[
            pltpu.VMEM((clips, half, depth), BF16),
            pltpu.VMEM((clips, count, depth), BF16),
            pltpu.SemaphoreType.DMA((clips * 2,)),
        ],
        compiler_params=params(24),
    )(own, partner, combine)


def solution(mesh):
    fine = Mesh(np.asarray(mesh.devices).reshape(4, 4, LINE, CORES), ("x", "z", "y", "core"))
    in_specs = (
        P(("x", "z"), ("y", "core"), None),
        P(),
        P(("x", "z", "y", "core"), None, None),
        P(("x", "z", "y", "core"), None, None),
    )
    out_specs = P(("x", "z"), ("y", "core"), None)
    return jax.shard_map(shards, mesh=fine, in_specs=in_specs, out_specs=out_specs, check_vma=False)
```

```python
import functools

import jax
import jax.numpy as jnp
import numpy as np
from jax import lax
from jax.experimental import pallas as pl
from jax.experimental.pallas import tpu as pltpu
from jax.sharding import Mesh
from jax.sharding import PartitionSpec as P

F32, BF16 = jnp.float32, jnp.bfloat16
STAT = 128
CHIPS, PLACES, LINE, CORES = 64, 16, 4, 2
MIB = 1024 * 1024


def iota(shape, dim):
    return lax.broadcasted_iota(jnp.int32, shape, dim)


def pieces(value, count):
    out = []
    for _ in range(count):
        part = value.astype(BF16).astype(F32)
        out.append(part)
        value = value - part
    return out


def read_stats(stats):
    return stats[:, 0:1] + stats[:, 1:2] + stats[:, 2:3], stats[:, 3:4] + stats[:, 4:5]


def interleave(rows, back):
    new = iota((rows, rows), 1 if back else 0)
    old = iota((rows, rows), 0 if back else 1)
    place = (new // 2) % 4 * (rows // 4) + new // 8 * 2 + new % 2
    return jnp.where(old == place, 1.0, 0.0).astype(BF16)


def stats_columns(logits):
    top = jnp.max(logits, axis=0, keepdims=True)
    exponent = jnp.exp(logits - top)
    total = jnp.sum(exponent, axis=0, keepdims=True)
    rows = pieces(top, 3) + pieces(total, 2) + [1.0 / total]
    rows.append(jnp.zeros((STAT - len(rows), logits.shape[1]), F32))
    return exponent.astype(BF16), jnp.concatenate(rows, axis=0).T


def store_sums(out_ref, c, exponent, stats, tokens):
    depth = tokens.shape[1]
    value = lax.dot_general(exponent, tokens, (((0,), (0,)), ((), ())), preferred_element_type=F32)
    out_ref[c, :, :depth] = (value * stats[:, 5:6]).astype(BF16)
    out_ref[c, :, depth:] = stats.astype(BF16)


def scores(tokens_ref, ordered_ref, other_ref, logits_ref, first):
    clips, _, slots = logits_ref.shape
    half = slots // CORES
    for c in range(clips):
        logits_ref[c] = jnp.dot(tokens_ref[first + c], ordered_ref[...], preferred_element_type=F32)
    for c in range(clips):
        store_sums(other_ref, c, *stats_columns(logits_ref[c, :, half:]), tokens_ref[first + c])


def first_scores_kernel(
    core_ref, tokens_hbm, router_hbm, other_ref, tokens_ref, logits_ref, ordered_ref, router_ref, sems
):
    clips = tokens_ref.shape[0]
    now = logits_ref.shape[0]
    slots = router_ref.shape[1]
    half = slots // CORES
    fetches = [pltpu.make_async_copy(tokens_hbm.at[c], tokens_ref.at[c], sems.at[c]) for c in range(clips)]
    fetch = pltpu.make_async_copy(router_hbm, router_ref, sems.at[clips])
    fetch.start()
    for copy in fetches[:now]:
        copy.start()
    row, column = iota((slots, slots), 0), iota((slots, slots), 1)
    core = core_ref[0]
    owner = jnp.where(column < half, core, 1 - core)
    within = column % half
    source = within // 2 * 4 + owner * 2 + within % 2
    chosen = jnp.where(row == source, 1.0, 0.0).astype(BF16)
    fetch.wait()
    for copy in fetches[now:]:
        copy.start()
    ordered_ref[...] = jnp.dot(router_ref[...], chosen, preferred_element_type=F32).astype(BF16)
    for copy in fetches[:now]:
        copy.wait()
    scores(tokens_ref, ordered_ref, other_ref, logits_ref, 0)
    for copy in fetches[now:]:
        copy.wait()


def last_scores_kernel(tokens_ref, ordered_ref, other_ref, logits_ref):
    scores(tokens_ref, ordered_ref, other_ref, logits_ref, tokens_ref.shape[0] - logits_ref.shape[0])


def sums_kernel(tokens_ref, first_ref, last_ref, mine_ref, combine_ref):
    half = mine_ref.shape[1]
    now = first_ref.shape[0]
    for c in range(tokens_ref.shape[0]):
        logits = first_ref[c] if c < now else last_ref[c - now]
        store_sums(mine_ref, c, *stats_columns(logits[:, :half]), tokens_ref[c])
        exponent = jnp.exp(logits - jnp.max(logits, axis=1, keepdims=True))
        combine_ref[c] = (exponent * (1.0 / jnp.sum(exponent, axis=1, keepdims=True))).astype(BF16)


def merge_kernel(mine_ref, first_ref, last_ref, out_ref):
    clips, half, width = mine_ref.shape
    depth = width - STAT
    rows, part = 256, 256 // clips
    order = interleave(rows, False)
    for group in range(half // part):
        at = slice(group * part, group * part + part)
        to = slice(group * rows // 8, (group + 1) * rows // 8)

        def load(lo, hi, *refs):
            return jnp.concatenate([ref[:, at, lo:hi] for ref in refs]).astype(F32).reshape(rows, hi - lo)

        def store(lo, hi, value):
            moved = jnp.dot(order, value.astype(BF16), preferred_element_type=F32)
            out_ref[to, :, lo:hi] = moved.reshape(rows // 8, 8, hi - lo).astype(BF16)

        top_a, total_a = read_stats(load(depth, width, mine_ref))
        top_b, total_b = read_stats(load(depth, width, first_ref, last_ref))
        top = jnp.maximum(top_a, top_b)
        weight_a = total_a * jnp.exp(top_a - top)
        weight_b = total_b * jnp.exp(top_b - top)
        total = weight_a + weight_b
        inverse = 1.0 / total
        lane = iota((rows, STAT), 1)
        stats = jnp.zeros((rows, STAT), F32)
        for k, value in enumerate(pieces(top, 3) + pieces(total, 2)):
            stats = jnp.where(lane == k, value, stats)
        store(depth, width, stats)
        weight_a, weight_b = weight_a * inverse, weight_b * inverse
        for lo in range(0, depth, 256):
            hi = lo + 256
            store(lo, hi, load(lo, hi, mine_ref) * weight_a + load(lo, hi, first_ref, last_ref) * weight_b)


def expert_kernel(tile, received_ref, up_ref, down_ref, out_ref, rows_ref, hidden_ref):
    depth, hidden = up_ref.shape[1:]
    for place in range(PLACES):
        parts = [received_ref[place * LINE + y].astype(F32) for y in range(LINE)]
        stats = [read_stats(part[:, depth:]) for part in parts]
        top = functools.reduce(jnp.maximum, [s[0] for s in stats])
        weights = [s[1] * jnp.exp(s[0] - top) for s in stats]
        inverse = 1.0 / sum(weights)
        rows_ref[place * 8:place * 8 + 8, :] = sum(
            part[:, :depth] * (weight * inverse) for part, weight in zip(parts, weights)
        )
    rows = rows_ref[...].astype(BF16)
    for lo in range(0, hidden, 2 * tile):
        hi = lo + 2 * tile
        value = jnp.dot(rows, up_ref[0, :, lo:hi], preferred_element_type=F32)
        hidden_ref[:, lo:hi] = (0.5 * value * (1.0 + lax.erf(value * np.float32(np.sqrt(0.5))))).astype(BF16)
    for lo in range(0, depth, tile):
        hi = lo + tile
        result = jnp.dot(hidden_ref[...], down_ref[0, :, lo:hi], preferred_element_type=F32)
        result = result.reshape(PLACES, 8, tile).astype(BF16)
        for place in range(PLACES):
            for y in range(LINE):
                out_ref[place * LINE + y, :, lo:hi] = result[place]


def by_clip(ref, out_ref):
    chips, lines, depth = ref.shape
    rows = 256
    order = interleave(rows, True)
    clips, part = 4, rows // 4
    for group in range(chips * lines // rows):
        for lo in range(0, depth, 256):
            block = ref[group * rows // 8:(group + 1) * rows // 8, :, lo:lo + 256]
            block = block.astype(F32).reshape(rows, 256).astype(BF16)
            moved = jnp.dot(order, block, preferred_element_type=F32).astype(BF16)
            out_ref[:, group * part:group * part + part, lo:lo + 256] = moved.reshape(clips, part, 256)


def mix_kernel(tile, mine_ref, theirs_ref, combine_ref, out_hbm, slots_ref, out_ref, sems):
    by_clip(theirs_ref, slots_ref)
    copies = []
    for c in range(combine_ref.shape[0]):
        slots = jnp.concatenate([mine_ref[c], slots_ref[c]], axis=0)
        for lo in range(0, combine_ref.shape[1], tile):
            out_ref[c, lo:lo + tile] = jnp.dot(
                combine_ref[c, lo:lo + tile], slots, preferred_element_type=F32
            ).astype(BF16)
            at = pl.ds(lo, tile)
            copy = pltpu.make_async_copy(out_ref.at[c, at], out_hbm.at[c, at], sems.at[len(copies)])
            copy.start()
            copies.append(copy)
    for copy in copies:
        copy.wait()


def in_hbm(array):
    return pltpu.with_memory_space_constraint(array, pltpu.HBM)


def params(mib):
    return pltpu.CompilerParams(vmem_limit_bytes=mib * MIB)


def shards(tokens, router, expert_up, expert_down):
    clips, count, depth = tokens.shape
    slots = router.shape[1]
    half = slots // CORES
    wide = depth + STAT
    core = lax.axis_index("core").astype(jnp.int32).reshape(1)
    swap = [(0, 1), (1, 0)]
    chips = ("x", "z", "y")

    whole = pl.BlockSpec(memory_space=pltpu.VMEM)
    far = pl.BlockSpec(memory_space=pltpu.HBM)

    now = 2
    near_shape = jax.ShapeDtypeStruct((clips, count, depth), BF16)
    ordered_shape = jax.ShapeDtypeStruct((depth, slots), BF16)

    def part(amount):
        return [
            jax.ShapeDtypeStruct((amount, half, wide), BF16),
            jax.ShapeDtypeStruct((amount, count, slots), F32),
        ]

    other, logits = part(now)
    first_other, near, first_logits, ordered = pl.pallas_call(
        first_scores_kernel,
        in_specs=[pl.BlockSpec(memory_space=pltpu.SMEM), far, far],
        out_specs=[whole] * 4,
        out_shape=[other, near_shape, logits, ordered_shape],
        scratch_shapes=[pltpu.VMEM((depth, slots), BF16), pltpu.SemaphoreType.DMA((clips + 1,))],
        compiler_params=params(36),
    )(core, in_hbm(tokens), in_hbm(router))
    first_theirs = lax.ppermute(first_other, "core", swap)

    last_other, last_logits = pl.pallas_call(
        last_scores_kernel,
        in_specs=[whole] * 2,
        out_specs=[whole] * 2,
        out_shape=part(clips - now),
        compiler_params=params(16),
    )(near, ordered)
    last_theirs = lax.ppermute(last_other, "core", swap)

    mine, combine = pl.pallas_call(
        sums_kernel,
        in_specs=[whole] * 3,
        out_specs=[whole] * 2,
        out_shape=[
            jax.ShapeDtypeStruct((clips, half, wide), BF16),
            jax.ShapeDtypeStruct((clips, count, slots), BF16),
        ],
        compiler_params=params(16),
    )(near, first_logits, last_logits)

    merged = pl.pallas_call(
        merge_kernel,
        in_specs=[whole] * 3,
        out_specs=whole,
        out_shape=jax.ShapeDtypeStruct((CHIPS, 8, wide), BF16),
        compiler_params=params(16),
    )(mine, first_theirs, last_theirs)

    received = lax.all_to_all(merged, chips, 0, 0, tiled=False)

    results = pl.pallas_call(
        functools.partial(expert_kernel, 256),
        in_specs=[whole] * 3,
        out_specs=whole,
        out_shape=jax.ShapeDtypeStruct((CHIPS, 8, depth), BF16),
        scratch_shapes=[pltpu.VMEM((PLACES * 8, depth), F32), pltpu.VMEM((PLACES * 8, expert_up.shape[2]), BF16)],
        compiler_params=params(32),
    )(received, expert_up, expert_down)

    returned = lax.all_to_all(results, chips, 0, 0, tiled=False)
    partner = lax.ppermute(returned, "core", swap)

    own = pl.pallas_call(
        by_clip,
        in_specs=[whole],
        out_specs=whole,
        out_shape=jax.ShapeDtypeStruct((clips, half, depth), BF16),
        compiler_params=params(16),
    )(returned)

    tile = count // 2
    return pl.pallas_call(
        functools.partial(mix_kernel, tile),
        in_specs=[whole] * 3,
        out_specs=far,
        out_shape=jax.ShapeDtypeStruct((clips, count, depth), BF16),
        scratch_shapes=[
            pltpu.VMEM((clips, half, depth), BF16),
            pltpu.VMEM((clips, count, depth), BF16),
            pltpu.SemaphoreType.DMA((clips * 2,)),
        ],
        compiler_params=params(24),
    )(own, partner, combine)


def solution(mesh):
    fine = Mesh(np.asarray(mesh.devices).reshape(4, 4, LINE, CORES), ("x", "z", "y", "core"))
    in_specs = (
        P(("x", "z"), ("y", "core"), None),
        P(),
        P(("x", "z", "y", "core"), None, None),
        P(("x", "z", "y", "core"), None, None),
    )
    out_specs = P(("x", "z"), ("y", "core"), None)
    return jax.shard_map(shards, mesh=fine, in_specs=in_specs, out_specs=out_specs, check_vma=False)
```

```python
import functools

import jax
import jax.numpy as jnp
import numpy as np
from jax import lax
from jax.experimental import pallas as pl
from jax.experimental.pallas import tpu as pltpu
from jax.sharding import Mesh
from jax.sharding import PartitionSpec as P

F32, BF16 = jnp.float32, jnp.bfloat16
STAT = 128
CHIPS, PLACES, LINE, CORES = 64, 16, 4, 2
MIB = 1024 * 1024


def iota(shape, dim):
    return lax.broadcasted_iota(jnp.int32, shape, dim)


def pieces(value, count):
    out = []
    for _ in range(count):
        part = value.astype(BF16).astype(F32)
        out.append(part)
        value = value - part
    return out


def read_stats(stats):
    return stats[:, 0:1] + stats[:, 1:2] + stats[:, 2:3], stats[:, 3:4] + stats[:, 4:5]


def interleave(rows, back):
    new = iota((rows, rows), 1 if back else 0)
    old = iota((rows, rows), 0 if back else 1)
    place = (new // 2) % 4 * (rows // 4) + new // 8 * 2 + new % 2
    return jnp.where(old == place, 1.0, 0.0).astype(BF16)


def stats_columns(logits):
    top = jnp.max(logits, axis=0, keepdims=True)
    exponent = jnp.exp(logits - top)
    total = jnp.sum(exponent, axis=0, keepdims=True)
    rows = pieces(top, 3) + pieces(total, 2) + [1.0 / total]
    rows.append(jnp.zeros((STAT - len(rows), logits.shape[1]), F32))
    return exponent.astype(BF16), jnp.concatenate(rows, axis=0).T


def store_sums(out_ref, c, exponent, stats, tokens):
    depth = tokens.shape[1]
    value = lax.dot_general(exponent, tokens, (((0,), (0,)), ((), ())), preferred_element_type=F32)
    out_ref[c, :, :depth] = (value * stats[:, 5:6]).astype(BF16)
    out_ref[c, :, depth:] = stats.astype(BF16)


def scores(tokens_ref, ordered_ref, other_ref, logits_ref, first):
    clips, _, slots = logits_ref.shape
    half = slots // CORES
    for c in range(clips):
        logits_ref[c] = jnp.dot(tokens_ref[first + c], ordered_ref[...], preferred_element_type=F32)
    for c in range(clips):
        store_sums(other_ref, c, *stats_columns(logits_ref[c, :, half:]), tokens_ref[first + c])


def first_scores_kernel(
    core_ref, tokens_hbm, router_hbm, other_ref, tokens_ref, logits_ref, ordered_ref, router_ref, sems
):
    clips = tokens_ref.shape[0]
    now = logits_ref.shape[0]
    slots = router_ref.shape[1]
    half = slots // CORES
    fetches = [pltpu.make_async_copy(tokens_hbm.at[c], tokens_ref.at[c], sems.at[c]) for c in range(clips)]
    fetch = pltpu.make_async_copy(router_hbm, router_ref, sems.at[clips])
    fetch.start()
    for copy in fetches[:now]:
        copy.start()
    row, column = iota((slots, slots), 0), iota((slots, slots), 1)
    core = core_ref[0]
    owner = jnp.where(column < half, core, 1 - core)
    within = column % half
    source = within // 2 * 4 + owner * 2 + within % 2
    chosen = jnp.where(row == source, 1.0, 0.0).astype(BF16)
    fetch.wait()
    for copy in fetches[now:]:
        copy.start()
    ordered_ref[...] = jnp.dot(router_ref[...], chosen, preferred_element_type=F32).astype(BF16)
    for copy in fetches[:now]:
        copy.wait()
    scores(tokens_ref, ordered_ref, other_ref, logits_ref, 0)
    for copy in fetches[now:]:
        copy.wait()


def last_scores_kernel(tokens_ref, ordered_ref, other_ref, logits_ref):
    scores(tokens_ref, ordered_ref, other_ref, logits_ref, tokens_ref.shape[0] - logits_ref.shape[0])


def sums_kernel(tokens_ref, first_ref, last_ref, mine_ref):
    half = mine_ref.shape[1]
    now = first_ref.shape[0]
    for c in range(tokens_ref.shape[0]):
        logits = first_ref[c, :, :half] if c < now else last_ref[c - now, :, :half]
        store_sums(mine_ref, c, *stats_columns(logits), tokens_ref[c])


def merge_kernel(mine_ref, first_ref, last_ref, out_ref):
    clips, half, width = mine_ref.shape
    depth = width - STAT
    rows, part = 256, 256 // clips
    order = interleave(rows, False)
    for group in range(half // part):
        at = slice(group * part, group * part + part)
        to = slice(group * rows // 8, (group + 1) * rows // 8)

        def load(lo, hi, *refs):
            return jnp.concatenate([ref[:, at, lo:hi] for ref in refs]).astype(F32).reshape(rows, hi - lo)

        def store(lo, hi, value):
            moved = jnp.dot(order, value.astype(BF16), preferred_element_type=F32)
            out_ref[to, :, lo:hi] = moved.reshape(rows // 8, 8, hi - lo).astype(BF16)

        top_a, total_a = read_stats(load(depth, width, mine_ref))
        top_b, total_b = read_stats(load(depth, width, first_ref, last_ref))
        top = jnp.maximum(top_a, top_b)
        weight_a = total_a * jnp.exp(top_a - top)
        weight_b = total_b * jnp.exp(top_b - top)
        total = weight_a + weight_b
        inverse = 1.0 / total
        lane = iota((rows, STAT), 1)
        stats = jnp.zeros((rows, STAT), F32)
        for k, value in enumerate(pieces(top, 3) + pieces(total, 2)):
            stats = jnp.where(lane == k, value, stats)
        store(depth, width, stats)
        weight_a, weight_b = weight_a * inverse, weight_b * inverse
        for lo in range(0, depth, 256):
            hi = lo + 256
            store(lo, hi, load(lo, hi, mine_ref) * weight_a + load(lo, hi, first_ref, last_ref) * weight_b)


def expert_kernel(tile, received_ref, up_ref, down_ref, out_ref, rows_ref, hidden_ref):
    depth, hidden = up_ref.shape[1:]
    for place in range(PLACES):
        parts = [received_ref[place * LINE + y].astype(F32) for y in range(LINE)]
        stats = [read_stats(part[:, depth:]) for part in parts]
        top = functools.reduce(jnp.maximum, [s[0] for s in stats])
        weights = [s[1] * jnp.exp(s[0] - top) for s in stats]
        inverse = 1.0 / sum(weights)
        rows_ref[place * 8:place * 8 + 8, :] = sum(
            part[:, :depth] * (weight * inverse) for part, weight in zip(parts, weights)
        )
    rows = rows_ref[...].astype(BF16)
    for lo in range(0, hidden, 2 * tile):
        hi = lo + 2 * tile
        value = jnp.dot(rows, up_ref[0, :, lo:hi], preferred_element_type=F32)
        hidden_ref[:, lo:hi] = (0.5 * value * (1.0 + lax.erf(value * np.float32(np.sqrt(0.5))))).astype(BF16)
    for lo in range(0, depth, tile):
        hi = lo + tile
        result = jnp.dot(hidden_ref[...], down_ref[0, :, lo:hi], preferred_element_type=F32)
        result = result.reshape(PLACES, 8, tile).astype(BF16)
        for place in range(PLACES):
            for y in range(LINE):
                out_ref[place * LINE + y, :, lo:hi] = result[place]


def by_clip(ref, out_ref):
    chips, lines, depth = ref.shape
    rows = 256
    order = interleave(rows, True)
    clips, part = 4, rows // 4
    for group in range(chips * lines // rows):
        for lo in range(0, depth, 256):
            block = ref[group * rows // 8:(group + 1) * rows // 8, :, lo:lo + 256]
            block = block.astype(F32).reshape(rows, 256).astype(BF16)
            moved = jnp.dot(order, block, preferred_element_type=F32).astype(BF16)
            out_ref[:, group * part:group * part + part, lo:lo + 256] = moved.reshape(clips, part, 256)


def window_kernel(mine_ref, first_ref, last_ref, slots_ref, combine_ref):
    by_clip(mine_ref, slots_ref)
    now = first_ref.shape[0]
    for c in range(combine_ref.shape[0]):
        logits = first_ref[c] if c < now else last_ref[c - now]
        exponent = jnp.exp(logits - jnp.max(logits, axis=1, keepdims=True))
        combine_ref[c] = (exponent * (1.0 / jnp.sum(exponent, axis=1, keepdims=True))).astype(BF16)


def mix_kernel(tile, mine_ref, theirs_ref, combine_ref, out_hbm, slots_ref, out_ref, sems):
    by_clip(theirs_ref, slots_ref)
    copies = []
    for c in range(combine_ref.shape[0]):
        slots = jnp.concatenate([mine_ref[c], slots_ref[c]], axis=0)
        for lo in range(0, combine_ref.shape[1], tile):
            out_ref[c, lo:lo + tile] = jnp.dot(
                combine_ref[c, lo:lo + tile], slots, preferred_element_type=F32
            ).astype(BF16)
            at = pl.ds(lo, tile)
            copy = pltpu.make_async_copy(out_ref.at[c, at], out_hbm.at[c, at], sems.at[len(copies)])
            copy.start()
            copies.append(copy)
    for copy in copies:
        copy.wait()


def in_hbm(array):
    return pltpu.with_memory_space_constraint(array, pltpu.HBM)


def params(mib):
    return pltpu.CompilerParams(vmem_limit_bytes=mib * MIB)


def shards(tokens, router, expert_up, expert_down):
    clips, count, depth = tokens.shape
    slots = router.shape[1]
    half = slots // CORES
    wide = depth + STAT
    core = lax.axis_index("core").astype(jnp.int32).reshape(1)
    swap = [(0, 1), (1, 0)]
    chips = ("x", "z", "y")

    whole = pl.BlockSpec(memory_space=pltpu.VMEM)
    far = pl.BlockSpec(memory_space=pltpu.HBM)

    now = 2
    near_shape = jax.ShapeDtypeStruct((clips, count, depth), BF16)
    ordered_shape = jax.ShapeDtypeStruct((depth, slots), BF16)

    def part(amount):
        return [
            jax.ShapeDtypeStruct((amount, half, wide), BF16),
            jax.ShapeDtypeStruct((amount, count, slots), F32),
        ]

    other, logits = part(now)
    first_other, near, first_logits, ordered = pl.pallas_call(
        first_scores_kernel,
        in_specs=[pl.BlockSpec(memory_space=pltpu.SMEM), far, far],
        out_specs=[whole] * 4,
        out_shape=[other, near_shape, logits, ordered_shape],
        scratch_shapes=[pltpu.VMEM((depth, slots), BF16), pltpu.SemaphoreType.DMA((clips + 1,))],
        compiler_params=params(36),
    )(core, in_hbm(tokens), in_hbm(router))
    first_theirs = lax.ppermute(first_other, "core", swap)

    last_other, last_logits = pl.pallas_call(
        last_scores_kernel,
        in_specs=[whole] * 2,
        out_specs=[whole] * 2,
        out_shape=part(clips - now),
        compiler_params=params(16),
    )(near, ordered)
    last_theirs = lax.ppermute(last_other, "core", swap)

    mine = pl.pallas_call(
        sums_kernel,
        in_specs=[whole] * 3,
        out_specs=whole,
        out_shape=jax.ShapeDtypeStruct((clips, half, wide), BF16),
        compiler_params=params(16),
    )(near, first_logits, last_logits)

    merged = pl.pallas_call(
        merge_kernel,
        in_specs=[whole] * 3,
        out_specs=whole,
        out_shape=jax.ShapeDtypeStruct((CHIPS, 8, wide), BF16),
        compiler_params=params(16),
    )(mine, first_theirs, last_theirs)

    received = lax.all_to_all(merged, chips, 0, 0, tiled=False)

    results = pl.pallas_call(
        functools.partial(expert_kernel, 256),
        in_specs=[whole] * 3,
        out_specs=whole,
        out_shape=jax.ShapeDtypeStruct((CHIPS, 8, depth), BF16),
        scratch_shapes=[pltpu.VMEM((PLACES * 8, depth), F32), pltpu.VMEM((PLACES * 8, expert_up.shape[2]), BF16)],
        compiler_params=params(32),
    )(received, expert_up, expert_down)

    returned = lax.all_to_all(results, chips, 0, 0, tiled=False)
    partner = lax.ppermute(returned, "core", swap)

    own, combine = pl.pallas_call(
        window_kernel,
        in_specs=[whole] * 3,
        out_specs=[whole] * 2,
        out_shape=[
            jax.ShapeDtypeStruct((clips, half, depth), BF16),
            jax.ShapeDtypeStruct((clips, count, slots), BF16),
        ],
        compiler_params=params(16),
    )(returned, first_logits, last_logits)

    tile = count // 4
    return pl.pallas_call(
        functools.partial(mix_kernel, tile),
        in_specs=[whole] * 3,
        out_specs=far,
        out_shape=jax.ShapeDtypeStruct((clips, count, depth), BF16),
        scratch_shapes=[
            pltpu.VMEM((clips, half, depth), BF16),
            pltpu.VMEM((clips, count, depth), BF16),
            pltpu.SemaphoreType.DMA((clips * 4,)),
        ],
        compiler_params=params(24),
    )(own, partner, combine)


def solution(mesh):
    fine = Mesh(np.asarray(mesh.devices).reshape(4, 4, LINE, CORES), ("x", "z", "y", "core"))
    in_specs = (
        P(("x", "z"), ("y", "core"), None),
        P(),
        P(("x", "z", "y", "core"), None, None),
        P(("x", "z", "y", "core"), None, None),
    )
    out_specs = P(("x", "z"), ("y", "core"), None)
    return jax.shard_map(shards, mesh=fine, in_specs=in_specs, out_specs=out_specs, check_vma=False)
```

```python
import functools

import jax
import jax.numpy as jnp
import numpy as np
from jax import lax
from jax.experimental import pallas as pl
from jax.experimental.pallas import tpu as pltpu
from jax.sharding import Mesh
from jax.sharding import PartitionSpec as P

F32, BF16 = jnp.float32, jnp.bfloat16
STAT = 128
CHIPS, PLACES, LINE, CORES = 64, 16, 4, 2
MIB = 1024 * 1024


def iota(shape, dim):
    return lax.broadcasted_iota(jnp.int32, shape, dim)


def pieces(value, count):
    out = []
    for _ in range(count):
        part = value.astype(BF16).astype(F32)
        out.append(part)
        value = value - part
    return out


def read_stats(stats):
    return stats[:, 0:1] + stats[:, 1:2] + stats[:, 2:3], stats[:, 3:4] + stats[:, 4:5]


def interleave(rows, back):
    new = iota((rows, rows), 1 if back else 0)
    old = iota((rows, rows), 0 if back else 1)
    place = (new // 2) % 4 * (rows // 4) + new // 8 * 2 + new % 2
    return jnp.where(old == place, 1.0, 0.0).astype(BF16)


def stats_columns(logits):
    top = jnp.max(logits, axis=0, keepdims=True)
    exponent = jnp.exp(logits - top)
    total = jnp.sum(exponent, axis=0, keepdims=True)
    rows = pieces(top, 3) + pieces(total, 2) + [1.0 / total]
    rows.append(jnp.zeros((STAT - len(rows), logits.shape[1]), F32))
    return exponent.astype(BF16), jnp.concatenate(rows, axis=0).T


def store_sums(out_ref, c, exponent, stats, tokens):
    depth = tokens.shape[1]
    value = lax.dot_general(exponent, tokens, (((0,), (0,)), ((), ())), preferred_element_type=F32)
    out_ref[c, :, :depth] = (value * stats[:, 5:6]).astype(BF16)
    out_ref[c, :, depth:] = stats.astype(BF16)


def scores(tokens_ref, ordered_ref, other_ref, logits_ref, first):
    clips, _, slots = logits_ref.shape
    half = slots // CORES
    for c in range(clips):
        logits_ref[c] = jnp.dot(tokens_ref[first + c], ordered_ref[...], preferred_element_type=F32)
    for c in range(clips):
        store_sums(other_ref, c, *stats_columns(logits_ref[c, :, half:]), tokens_ref[first + c])


def first_scores_kernel(
    core_ref, tokens_hbm, router_hbm, other_ref, tokens_ref, logits_ref, ordered_ref, router_ref, sems
):
    clips = tokens_ref.shape[0]
    now = logits_ref.shape[0]
    slots = router_ref.shape[1]
    half = slots // CORES
    fetches = [pltpu.make_async_copy(tokens_hbm.at[c], tokens_ref.at[c], sems.at[c]) for c in range(clips)]
    fetch = pltpu.make_async_copy(router_hbm, router_ref, sems.at[clips])
    fetch.start()
    for copy in fetches[:now]:
        copy.start()
    row, column = iota((slots, slots), 0), iota((slots, slots), 1)
    core = core_ref[0]
    owner = jnp.where(column < half, core, 1 - core)
    within = column % half
    source = within // 2 * 4 + owner * 2 + within % 2
    chosen = jnp.where(row == source, 1.0, 0.0).astype(BF16)
    fetch.wait()
    ordered_ref[...] = jnp.dot(router_ref[...], chosen, preferred_element_type=F32).astype(BF16)
    for copy in fetches[:now]:
        copy.wait()
    for copy in fetches[now:]:
        copy.start()
    scores(tokens_ref, ordered_ref, other_ref, logits_ref, 0)
    for copy in fetches[now:]:
        copy.wait()


def last_scores_kernel(tokens_ref, ordered_ref, other_ref, logits_ref):
    scores(tokens_ref, ordered_ref, other_ref, logits_ref, tokens_ref.shape[0] - logits_ref.shape[0])


def sums_kernel(tokens_ref, first_ref, last_ref, mine_ref, combine_ref):
    half = mine_ref.shape[1]
    now = first_ref.shape[0]
    for c in range(tokens_ref.shape[0]):
        logits = first_ref[c] if c < now else last_ref[c - now]
        store_sums(mine_ref, c, *stats_columns(logits[:, :half]), tokens_ref[c])
        exponent = jnp.exp(logits - jnp.max(logits, axis=1, keepdims=True))
        combine_ref[c] = (exponent * (1.0 / jnp.sum(exponent, axis=1, keepdims=True))).astype(BF16)


def merge_kernel(mine_ref, first_ref, last_ref, out_ref):
    clips, half, width = mine_ref.shape
    depth = width - STAT
    rows, part = 256, 256 // clips
    order = interleave(rows, False)
    for group in range(half // part):
        at = slice(group * part, group * part + part)
        to = slice(group * rows // 8, (group + 1) * rows // 8)

        def load(lo, hi, *refs):
            return jnp.concatenate([ref[:, at, lo:hi] for ref in refs]).astype(F32).reshape(rows, hi - lo)

        def store(lo, hi, value):
            moved = jnp.dot(order, value.astype(BF16), preferred_element_type=F32)
            out_ref[to, :, lo:hi] = moved.reshape(rows // 8, 8, hi - lo).astype(BF16)

        top_a, total_a = read_stats(load(depth, width, mine_ref))
        top_b, total_b = read_stats(load(depth, width, first_ref, last_ref))
        top = jnp.maximum(top_a, top_b)
        weight_a = total_a * jnp.exp(top_a - top)
        weight_b = total_b * jnp.exp(top_b - top)
        total = weight_a + weight_b
        inverse = 1.0 / total
        lane = iota((rows, STAT), 1)
        stats = jnp.zeros((rows, STAT), F32)
        for k, value in enumerate(pieces(top, 3) + pieces(total, 2)):
            stats = jnp.where(lane == k, value, stats)
        store(depth, width, stats)
        weight_a, weight_b = weight_a * inverse, weight_b * inverse
        for lo in range(0, depth, 256):
            hi = lo + 256
            store(lo, hi, load(lo, hi, mine_ref) * weight_a + load(lo, hi, first_ref, last_ref) * weight_b)


def expert_kernel(tile, received_ref, up_ref, down_ref, out_ref, rows_ref, hidden_ref):
    depth, hidden = up_ref.shape[1:]
    for place in range(PLACES):
        parts = [received_ref[place * LINE + y].astype(F32) for y in range(LINE)]
        stats = [read_stats(part[:, depth:]) for part in parts]
        top = functools.reduce(jnp.maximum, [s[0] for s in stats])
        weights = [s[1] * jnp.exp(s[0] - top) for s in stats]
        inverse = 1.0 / sum(weights)
        rows_ref[place * 8:place * 8 + 8, :] = sum(
            part[:, :depth] * (weight * inverse) for part, weight in zip(parts, weights)
        )
    rows = rows_ref[...].astype(BF16)
    for lo in range(0, hidden, 2 * tile):
        hi = lo + 2 * tile
        value = jnp.dot(rows, up_ref[0, :, lo:hi], preferred_element_type=F32)
        hidden_ref[:, lo:hi] = (0.5 * value * (1.0 + lax.erf(value * np.float32(np.sqrt(0.5))))).astype(BF16)
    for lo in range(0, depth, tile):
        hi = lo + tile
        result = jnp.dot(hidden_ref[...], down_ref[0, :, lo:hi], preferred_element_type=F32)
        result = result.reshape(PLACES, 8, tile).astype(BF16)
        for place in range(PLACES):
            for y in range(LINE):
                out_ref[place * LINE + y, :, lo:hi] = result[place]


def by_clip(ref, out_ref):
    chips, lines, depth = ref.shape
    rows = 256
    order = interleave(rows, True)
    clips, part = 4, rows // 4
    for group in range(chips * lines // rows):
        for lo in range(0, depth, 256):
            block = ref[group * rows // 8:(group + 1) * rows // 8, :, lo:lo + 256]
            block = block.astype(F32).reshape(rows, 256).astype(BF16)
            moved = jnp.dot(order, block, preferred_element_type=F32).astype(BF16)
            out_ref[:, group * part:group * part + part, lo:lo + 256] = moved.reshape(clips, part, 256)


def mix_kernel(tile, mine_ref, theirs_ref, combine_ref, out_hbm, slots_ref, out_ref, sems):
    by_clip(theirs_ref, slots_ref)
    copies = []
    for c in range(combine_ref.shape[0]):
        slots = jnp.concatenate([mine_ref[c], slots_ref[c]], axis=0)
        for lo in range(0, combine_ref.shape[1], tile):
            out_ref[c, lo:lo + tile] = jnp.dot(
                combine_ref[c, lo:lo + tile], slots, preferred_element_type=F32
            ).astype(BF16)
            at = pl.ds(lo, tile)
            copy = pltpu.make_async_copy(out_ref.at[c, at], out_hbm.at[c, at], sems.at[len(copies)])
            copy.start()
            copies.append(copy)
    for copy in copies:
        copy.wait()


def in_hbm(array):
    return pltpu.with_memory_space_constraint(array, pltpu.HBM)


def params(mib):
    return pltpu.CompilerParams(vmem_limit_bytes=mib * MIB)


def shards(tokens, router, expert_up, expert_down):
    clips, count, depth = tokens.shape
    slots = router.shape[1]
    half = slots // CORES
    wide = depth + STAT
    core = lax.axis_index("core").astype(jnp.int32).reshape(1)
    swap = [(0, 1), (1, 0)]
    chips = ("x", "z", "y")

    whole = pl.BlockSpec(memory_space=pltpu.VMEM)
    far = pl.BlockSpec(memory_space=pltpu.HBM)

    now = 2
    near_shape = jax.ShapeDtypeStruct((clips, count, depth), BF16)
    ordered_shape = jax.ShapeDtypeStruct((depth, slots), BF16)

    def part(amount):
        return [
            jax.ShapeDtypeStruct((amount, half, wide), BF16),
            jax.ShapeDtypeStruct((amount, count, slots), F32),
        ]

    other, logits = part(now)
    first_other, near, first_logits, ordered = pl.pallas_call(
        first_scores_kernel,
        in_specs=[pl.BlockSpec(memory_space=pltpu.SMEM), far, far],
        out_specs=[whole] * 4,
        out_shape=[other, near_shape, logits, ordered_shape],
        scratch_shapes=[pltpu.VMEM((depth, slots), BF16), pltpu.SemaphoreType.DMA((clips + 1,))],
        compiler_params=params(36),
    )(core, in_hbm(tokens), in_hbm(router))
    first_theirs = lax.ppermute(first_other, "core", swap)

    last_other, last_logits = pl.pallas_call(
        last_scores_kernel,
        in_specs=[whole] * 2,
        out_specs=[whole] * 2,
        out_shape=part(clips - now),
        compiler_params=params(16),
    )(near, ordered)
    last_theirs = lax.ppermute(last_other, "core", swap)

    mine, combine = pl.pallas_call(
        sums_kernel,
        in_specs=[whole] * 3,
        out_specs=[whole] * 2,
        out_shape=[
            jax.ShapeDtypeStruct((clips, half, wide), BF16),
            jax.ShapeDtypeStruct((clips, count, slots), BF16),
        ],
        compiler_params=params(16),
    )(near, first_logits, last_logits)

    merged = pl.pallas_call(
        merge_kernel,
        in_specs=[whole] * 3,
        out_specs=whole,
        out_shape=jax.ShapeDtypeStruct((CHIPS, 8, wide), BF16),
        compiler_params=params(16),
    )(mine, first_theirs, last_theirs)

    received = lax.all_to_all(merged, chips, 0, 0, tiled=False)

    results = pl.pallas_call(
        functools.partial(expert_kernel, 256),
        in_specs=[whole] * 3,
        out_specs=whole,
        out_shape=jax.ShapeDtypeStruct((CHIPS, 8, depth), BF16),
        scratch_shapes=[pltpu.VMEM((PLACES * 8, depth), F32), pltpu.VMEM((PLACES * 8, expert_up.shape[2]), BF16)],
        compiler_params=params(32),
    )(received, expert_up, expert_down)

    returned = lax.all_to_all(results, chips, 0, 0, tiled=False)
    partner = lax.ppermute(returned, "core", swap)

    own = pl.pallas_call(
        by_clip,
        in_specs=[whole],
        out_specs=whole,
        out_shape=jax.ShapeDtypeStruct((clips, half, depth), BF16),
        compiler_params=params(16),
    )(returned)

    tile = count // 2
    return pl.pallas_call(
        functools.partial(mix_kernel, tile),
        in_specs=[whole] * 3,
        out_specs=far,
        out_shape=jax.ShapeDtypeStruct((clips, count, depth), BF16),
        scratch_shapes=[
            pltpu.VMEM((clips, half, depth), BF16),
            pltpu.VMEM((clips, count, depth), BF16),
            pltpu.SemaphoreType.DMA((clips * 2,)),
        ],
        compiler_params=params(24),
    )(own, partner, combine)


def solution(mesh):
    fine = Mesh(np.asarray(mesh.devices).reshape(4, 4, LINE, CORES), ("x", "z", "y", "core"))
    in_specs = (
        P(("x", "z"), ("y", "core"), None),
        P(),
        P(("x", "z", "y", "core"), None, None),
        P(("x", "z", "y", "core"), None, None),
    )
    out_specs = P(("x", "z"), ("y", "core"), None)
    return jax.shard_map(shards, mesh=fine, in_specs=in_specs, out_specs=out_specs, check_vma=False)
```

```python
import functools

import jax
import jax.numpy as jnp
import numpy as np
from jax import lax
from jax.experimental import pallas as pl
from jax.experimental.pallas import tpu as pltpu
from jax.sharding import Mesh
from jax.sharding import PartitionSpec as P

F32, BF16 = jnp.float32, jnp.bfloat16
STAT = 128
CHIPS, PLACES, LINE, CORES = 64, 16, 4, 2
MIB = 1024 * 1024


def iota(shape, dim):
    return lax.broadcasted_iota(jnp.int32, shape, dim)


def pieces(value, count):
    out = []
    for _ in range(count):
        part = value.astype(BF16).astype(F32)
        out.append(part)
        value = value - part
    return out


def read_stats(stats):
    return stats[:, 0:1] + stats[:, 1:2] + stats[:, 2:3], stats[:, 3:4] + stats[:, 4:5]


def interleave(rows, back):
    new = iota((rows, rows), 1 if back else 0)
    old = iota((rows, rows), 0 if back else 1)
    place = (new // 2) % 4 * (rows // 4) + new // 8 * 2 + new % 2
    return jnp.where(old == place, 1.0, 0.0).astype(BF16)


def stats_columns(logits):
    top = jnp.max(logits, axis=0, keepdims=True)
    exponent = jnp.exp(logits - top)
    total = jnp.sum(exponent, axis=0, keepdims=True)
    rows = pieces(top, 3) + pieces(total, 2) + [1.0 / total]
    rows.append(jnp.zeros((STAT - len(rows), logits.shape[1]), F32))
    return exponent.astype(BF16), jnp.concatenate(rows, axis=0).T


def store_sums(out_ref, c, exponent, stats, tokens):
    depth = tokens.shape[1]
    value = lax.dot_general(exponent, tokens, (((0,), (0,)), ((), ())), preferred_element_type=F32)
    out_ref[c, :, :depth] = (value * stats[:, 5:6]).astype(BF16)
    out_ref[c, :, depth:] = stats.astype(BF16)


def scores(tokens_ref, ordered_ref, other_ref, logits_ref, first):
    clips, _, slots = logits_ref.shape
    half = slots // CORES
    for c in range(clips):
        logits_ref[c] = jnp.dot(tokens_ref[first + c], ordered_ref[...], preferred_element_type=F32)
    for c in range(clips):
        store_sums(other_ref, c, *stats_columns(logits_ref[c, :, half:]), tokens_ref[first + c])


def first_scores_kernel(
    core_ref, tokens_hbm, router_hbm, other_ref, tokens_ref, logits_ref, ordered_ref, router_ref, sems
):
    clips = tokens_ref.shape[0]
    now = logits_ref.shape[0]
    slots = router_ref.shape[1]
    half = slots // CORES
    fetches = [pltpu.make_async_copy(tokens_hbm.at[c], tokens_ref.at[c], sems.at[c]) for c in range(clips)]
    fetch = pltpu.make_async_copy(router_hbm, router_ref, sems.at[clips])
    fetch.start()
    for copy in fetches[:now]:
        copy.start()
    row, column = iota((slots, slots), 0), iota((slots, slots), 1)
    core = core_ref[0]
    owner = jnp.where(column < half, core, 1 - core)
    within = column % half
    source = within // 2 * 4 + owner * 2 + within % 2
    chosen = jnp.where(row == source, 1.0, 0.0).astype(BF16)
    fetch.wait()
    for copy in fetches[now:]:
        copy.start()
    ordered_ref[...] = jnp.dot(router_ref[...], chosen, preferred_element_type=F32).astype(BF16)
    for copy in fetches[:now]:
        copy.wait()
    scores(tokens_ref, ordered_ref, other_ref, logits_ref, 0)
    for copy in fetches[now:]:
        copy.wait()


def last_scores_kernel(tokens_ref, ordered_ref, other_ref, logits_ref):
    scores(tokens_ref, ordered_ref, other_ref, logits_ref, tokens_ref.shape[0] - logits_ref.shape[0])


def sums_kernel(tokens_ref, first_ref, last_ref, mine_ref):
    half = mine_ref.shape[1]
    now = first_ref.shape[0]
    for c in range(tokens_ref.shape[0]):
        logits = first_ref[c, :, :half] if c < now else last_ref[c - now, :, :half]
        store_sums(mine_ref, c, *stats_columns(logits), tokens_ref[c])


def merge_kernel(mine_ref, first_ref, last_ref, out_ref):
    clips, half, width = mine_ref.shape
    depth = width - STAT
    rows, part = 256, 256 // clips
    order = interleave(rows, False)
    for group in range(half // part):
        at = slice(group * part, group * part + part)
        to = slice(group * rows // 8, (group + 1) * rows // 8)

        def load(lo, hi, *refs):
            return jnp.concatenate([ref[:, at, lo:hi] for ref in refs]).astype(F32).reshape(rows, hi - lo)

        def store(lo, hi, value):
            moved = jnp.dot(order, value.astype(BF16), preferred_element_type=F32)
            out_ref[to, :, lo:hi] = moved.reshape(rows // 8, 8, hi - lo).astype(BF16)

        top_a, total_a = read_stats(load(depth, width, mine_ref))
        top_b, total_b = read_stats(load(depth, width, first_ref, last_ref))
        top = jnp.maximum(top_a, top_b)
        weight_a = total_a * jnp.exp(top_a - top)
        weight_b = total_b * jnp.exp(top_b - top)
        total = weight_a + weight_b
        inverse = 1.0 / total
        lane = iota((rows, STAT), 1)
        stats = jnp.zeros((rows, STAT), F32)
        for k, value in enumerate(pieces(top, 3) + pieces(total, 2)):
            stats = jnp.where(lane == k, value, stats)
        store(depth, width, stats)
        weight_a, weight_b = weight_a * inverse, weight_b * inverse
        for lo in range(0, depth, 256):
            hi = lo + 256
            store(lo, hi, load(lo, hi, mine_ref) * weight_a + load(lo, hi, first_ref, last_ref) * weight_b)


def expert_kernel(tile, received_ref, up_ref, down_ref, out_ref, rows_ref, hidden_ref):
    depth, hidden = up_ref.shape[1:]
    for place in range(PLACES):
        parts = [received_ref[place * LINE + y].astype(F32) for y in range(LINE)]
        stats = [read_stats(part[:, depth:]) for part in parts]
        top = functools.reduce(jnp.maximum, [s[0] for s in stats])
        weights = [s[1] * jnp.exp(s[0] - top) for s in stats]
        inverse = 1.0 / sum(weights)
        rows_ref[place * 8:place * 8 + 8, :] = sum(
            part[:, :depth] * (weight * inverse) for part, weight in zip(parts, weights)
        )
    rows = rows_ref[...].astype(BF16)
    for lo in range(0, hidden, 2 * tile):
        hi = lo + 2 * tile
        value = jnp.dot(rows, up_ref[0, :, lo:hi], preferred_element_type=F32)
        hidden_ref[:, lo:hi] = (0.5 * value * (1.0 + lax.erf(value * np.float32(np.sqrt(0.5))))).astype(BF16)
    for lo in range(0, depth, tile):
        hi = lo + tile
        result = jnp.dot(hidden_ref[...], down_ref[0, :, lo:hi], preferred_element_type=F32)
        result = result.reshape(PLACES, 8, tile).astype(BF16)
        for place in range(PLACES):
            for y in range(LINE):
                out_ref[place * LINE + y, :, lo:hi] = result[place]


def by_clip(ref, out_ref):
    chips, lines, depth = ref.shape
    rows = 256
    order = interleave(rows, True)
    clips, part = 4, rows // 4
    for group in range(chips * lines // rows):
        for lo in range(0, depth, 256):
            block = ref[group * rows // 8:(group + 1) * rows // 8, :, lo:lo + 256]
            block = block.astype(F32).reshape(rows, 256).astype(BF16)
            moved = jnp.dot(order, block, preferred_element_type=F32).astype(BF16)
            out_ref[:, group * part:group * part + part, lo:lo + 256] = moved.reshape(clips, part, 256)


def combine_kernel(first_ref, last_ref, combine_ref):
    now = first_ref.shape[0]
    for c in range(combine_ref.shape[0]):
        logits = first_ref[c] if c < now else last_ref[c - now]
        exponent = jnp.exp(logits - jnp.max(logits, axis=1, keepdims=True))
        combine_ref[c] = (exponent * (1.0 / jnp.sum(exponent, axis=1, keepdims=True))).astype(BF16)


def mix_kernel(tile, mine_ref, theirs_ref, combine_ref, out_hbm, slots_ref, out_ref, sems):
    by_clip(theirs_ref, slots_ref)
    copies = []
    for c in range(combine_ref.shape[0]):
        slots = jnp.concatenate([mine_ref[c], slots_ref[c]], axis=0)
        for lo in range(0, combine_ref.shape[1], tile):
            out_ref[c, lo:lo + tile] = jnp.dot(
                combine_ref[c, lo:lo + tile], slots, preferred_element_type=F32
            ).astype(BF16)
            at = pl.ds(lo, tile)
            copy = pltpu.make_async_copy(out_ref.at[c, at], out_hbm.at[c, at], sems.at[len(copies)])
            copy.start()
            copies.append(copy)
    for copy in copies:
        copy.wait()


def in_hbm(array):
    return pltpu.with_memory_space_constraint(array, pltpu.HBM)


def params(mib):
    return pltpu.CompilerParams(vmem_limit_bytes=mib * MIB)


def shards(tokens, router, expert_up, expert_down):
    clips, count, depth = tokens.shape
    slots = router.shape[1]
    half = slots // CORES
    wide = depth + STAT
    core = lax.axis_index("core").astype(jnp.int32).reshape(1)
    swap = [(0, 1), (1, 0)]
    chips = ("x", "z", "y")

    whole = pl.BlockSpec(memory_space=pltpu.VMEM)
    far = pl.BlockSpec(memory_space=pltpu.HBM)

    now = 2
    near_shape = jax.ShapeDtypeStruct((clips, count, depth), BF16)
    ordered_shape = jax.ShapeDtypeStruct((depth, slots), BF16)

    def part(amount):
        return [
            jax.ShapeDtypeStruct((amount, half, wide), BF16),
            jax.ShapeDtypeStruct((amount, count, slots), F32),
        ]

    other, logits = part(now)
    first_other, near, first_logits, ordered = pl.pallas_call(
        first_scores_kernel,
        in_specs=[pl.BlockSpec(memory_space=pltpu.SMEM), far, far],
        out_specs=[whole] * 4,
        out_shape=[other, near_shape, logits, ordered_shape],
        scratch_shapes=[pltpu.VMEM((depth, slots), BF16), pltpu.SemaphoreType.DMA((clips + 1,))],
        compiler_params=params(36),
    )(core, in_hbm(tokens), in_hbm(router))
    first_theirs = lax.ppermute(first_other, "core", swap)

    last_other, last_logits = pl.pallas_call(
        last_scores_kernel,
        in_specs=[whole] * 2,
        out_specs=[whole] * 2,
        out_shape=part(clips - now),
        compiler_params=params(16),
    )(near, ordered)
    last_theirs = lax.ppermute(last_other, "core", swap)

    mine = pl.pallas_call(
        sums_kernel,
        in_specs=[whole] * 3,
        out_specs=whole,
        out_shape=jax.ShapeDtypeStruct((clips, half, wide), BF16),
        compiler_params=params(16),
    )(near, first_logits, last_logits)

    merged = pl.pallas_call(
        merge_kernel,
        in_specs=[whole] * 3,
        out_specs=whole,
        out_shape=jax.ShapeDtypeStruct((CHIPS, 8, wide), BF16),
        compiler_params=params(16),
    )(mine, first_theirs, last_theirs)

    received = lax.all_to_all(merged, chips, 0, 0, tiled=False)

    combine = pl.pallas_call(
        combine_kernel,
        in_specs=[whole] * 2,
        out_specs=whole,
        out_shape=jax.ShapeDtypeStruct((clips, count, slots), BF16),
        compiler_params=params(16),
        cost_estimate=pl.CostEstimate(flops=4 * 10**6, bytes_accessed=4 * 10**6, transcendentals=7 * 10**5),
    )(first_logits, last_logits)

    results = pl.pallas_call(
        functools.partial(expert_kernel, 256),
        in_specs=[whole] * 3,
        out_specs=whole,
        out_shape=jax.ShapeDtypeStruct((CHIPS, 8, depth), BF16),
        scratch_shapes=[pltpu.VMEM((PLACES * 8, depth), F32), pltpu.VMEM((PLACES * 8, expert_up.shape[2]), BF16)],
        compiler_params=params(32),
    )(received, expert_up, expert_down)

    returned = lax.all_to_all(results, chips, 0, 0, tiled=False)
    partner = lax.ppermute(returned, "core", swap)

    own = pl.pallas_call(
        by_clip,
        in_specs=[whole],
        out_specs=whole,
        out_shape=jax.ShapeDtypeStruct((clips, half, depth), BF16),
        compiler_params=params(16),
    )(returned)

    tile = count // 4
    return pl.pallas_call(
        functools.partial(mix_kernel, tile),
        in_specs=[whole] * 3,
        out_specs=far,
        out_shape=jax.ShapeDtypeStruct((clips, count, depth), BF16),
        scratch_shapes=[
            pltpu.VMEM((clips, half, depth), BF16),
            pltpu.VMEM((clips, count, depth), BF16),
            pltpu.SemaphoreType.DMA((clips * 4,)),
        ],
        compiler_params=params(24),
    )(own, partner, combine)


def solution(mesh):
    fine = Mesh(np.asarray(mesh.devices).reshape(4, 4, LINE, CORES), ("x", "z", "y", "core"))
    in_specs = (
        P(("x", "z"), ("y", "core"), None),
        P(),
        P(("x", "z", "y", "core"), None, None),
        P(("x", "z", "y", "core"), None, None),
    )
    out_specs = P(("x", "z"), ("y", "core"), None)
    return jax.shard_map(shards, mesh=fine, in_specs=in_specs, out_specs=out_specs, check_vma=False)
```
